32 devices in a mesh: rep: 4 (over z), shard: 8 (over y, x, core).
Axes of the slice: x: 2, y: 2, z: 4, core: 2. Of those that a mesh axis runs over, the one named last changes fastest.
Arguments:
- trained_sq: float32 [4, 4, 768, 768], P('rep', None, 'shard'), may hold values from -6 to 6
- trained_up: float32 [4, 768, 3072], P('rep', 'shard'), may hold values from -6 to 6
- trained_down: float32 [4, 3072, 768], P('rep', 'shard'), may hold values from -6 to 6
- trained_ln: float32 [4, 4, 768], P('rep', None, 'shard'), may hold values from -6 to 6
- start_sq: float32 [4, 768, 768], P(None, 'shard'), may hold values from -6 to 6
- start_up: float32 [768, 3072], P('shard'), may hold values from -6 to 6
- start_down: float32 [3072, 768], P('shard'), may hold values from -6 to 6
- start_ln: float32 [4, 768], P(None, 'shard'), may hold values from -6 to 6
- resid_sq: float32 [4, 4, 768, 768], P('rep', None, 'shard'), may hold values from -4 to 4
- resid_up: float32 [4, 768, 3072], P('rep', 'shard'), may hold values from -4 to 4
- resid_down: float32 [4, 3072, 768], P('rep', 'shard'), may hold values from -4 to 4
- mom_sq: float32 [4, 768, 768], P(None, 'shard'), may hold values from -3 to 3
- mom_up: float32 [768, 3072], P('shard'), may hold values from -3 to 3
- mom_down: float32 [3072, 768], P('shard'), may hold values from -3 to 3
- mom_ln: float32 [4, 768], P(None, 'shard'), may hold values from -3 to 3
- basis_sq: float32 [4, 768, 64], replicated, may hold values from -0.21875 to 0.21875
- basis_up: float32 [3072, 64], replicated, may hold values from -0.109375 to 0.109375
- basis_down: float32 [768, 64], replicated, may hold values from -0.21875 to 0.21875
Outputs:
- new_resid_sq: float32 [4, 4, 768, 768], P('rep', None, 'shard')
- new_resid_up: float32 [4, 768, 3072], P('rep', 'shard')
- new_resid_down: float32 [4, 3072, 768], P('rep', 'shard')
- new_mom_sq: float32 [4, 768, 768], P(None, 'shard')
- new_mom_up: float32 [768, 3072], P('shard')
- new_mom_down: float32 [3072, 768], P('shard')
- new_mom_ln: float32 [4, 768], P(None, 'shard')
- weights_sq: bfloat16 [4, 768, 768], replicated
- weights_up: bfloat16 [768, 3072], replicated
- weights_down: bfloat16 [3072, 768], replicated
- weights_ln: bfloat16 [4, 768], replicated
The draws below stay inside these ranges and needn't reach their ends.
All inputs are finite; a program needn't handle non-finite values.
Results may differ from the reference program's by a relative error of at most 0.001.
Values may be sent and summed in bfloat16 or wider, within the bound.
A program may use at most 128 MiB of HBM per device.

```python
import jax
import jax.numpy as jnp
from jax import lax

D = 768
FF = 3072
RANK = 64
SQUARE = 4
GROUPS = 4


def levels(stream_key, shape, cuts, smallest, top_value):
    gain, own = 1.0, jax.random.fold_in(stream_key, 6)
    for dim, blocks in cuts:
        steps = jnp.exp(jax.random.uniform(jax.random.fold_in(own, dim), (blocks,), jnp.float32, smallest / len(cuts), top_value / len(cuts)))
        gain = gain * jnp.repeat(steps, shape[dim] // blocks).reshape([-1 if axis == dim else 1 for axis in range(len(shape))])
    return gain


def scatter_about(key, dims, deviation, bound, shards=(), held_as=jnp.bfloat16):
    array = deviation * jax.random.normal(key, dims, jnp.float32)
    if shards:
        array = array * levels(key, dims, shards, -0.22, 0.18)
    return jnp.clip(array, -bound, bound).astype(held_as)


def setup_inputs(seed: int = 0) -> dict:
    key_of = jax.random.split(jax.random.key(seed), 19)
    return {
        "trained_sq": scatter_about(key_of[0], (GROUPS, SQUARE, D, D), 1.0, 6.0, ((0, 4), (2, 8)), jnp.float32),
        "trained_up": scatter_about(key_of[1], (GROUPS, D, FF), 1.0, 6.0, ((0, 4), (1, 8)), jnp.float32),
        "trained_down": scatter_about(key_of[2], (GROUPS, FF, D), 1.0, 6.0, ((0, 4), (1, 8)), jnp.float32),
        "trained_ln": scatter_about(key_of[3], (GROUPS, 4, D), 1.0, 6.0, ((0, 4), (2, 8)), jnp.float32),
        "start_sq": scatter_about(key_of[4], (SQUARE, D, D), 1.0, 6.0, ((1, 8),), jnp.float32),
        "start_up": scatter_about(key_of[5], (D, FF), 1.0, 6.0, ((0, 8),), jnp.float32),
        "start_down": scatter_about(key_of[6], (FF, D), 1.0, 6.0, ((0, 8),), jnp.float32),
        "start_ln": scatter_about(key_of[7], (4, D), 1.0, 6.0, ((1, 8),), jnp.float32),
        "resid_sq": scatter_about(key_of[8], (GROUPS, SQUARE, D, D), 0.5, 4.0, ((0, 4), (2, 8)), jnp.float32),
        "resid_up": scatter_about(key_of[9], (GROUPS, D, FF), 0.5, 4.0, ((0, 4), (1, 8)), jnp.float32),
        "resid_down": scatter_about(key_of[10], (GROUPS, FF, D), 0.5, 4.0, ((0, 4), (1, 8)), jnp.float32),
        "mom_sq": scatter_about(key_of[11], (SQUARE, D, D), 0.3, 3.0, ((1, 8),), jnp.float32),
        "mom_up": scatter_about(key_of[12], (D, FF), 0.3, 3.0, ((0, 8),), jnp.float32),
        "mom_down": scatter_about(key_of[13], (FF, D), 0.3, 3.0, ((0, 8),), jnp.float32),
        "mom_ln": scatter_about(key_of[14], (4, D), 0.3, 3.0, ((1, 8),), jnp.float32),
        "basis_sq": scatter_about(key_of[15], (SQUARE, D, RANK), D ** -0.5, 0.21875, (), jnp.float32),
        "basis_up": scatter_about(key_of[16], (FF, RANK), FF ** -0.5, 0.109375, (), jnp.float32),
        "basis_down": scatter_about(key_of[17], (D, RANK), D ** -0.5, 0.21875, (), jnp.float32),
    }


moment_coef = 0.9
outer_rate = 0.7


def advance(start, moment, outer):
    new_moment = moment_coef * moment + outer
    weights = (start - outer_rate * (outer + moment_coef * new_moment)).astype(jnp.bfloat16)
    return new_moment, weights


def reference(trained_sq, trained_up, trained_down, trained_ln, start_sq, start_up, start_down, start_ln, resid_sq, resid_up, resid_down, mom_sq, mom_up, mom_down, mom_ln, basis_sq, basis_up, basis_down):
    highest = lax.Precision.HIGHEST
    delta_sq = start_sq[None] - trained_sq + resid_sq
    factor_sq = jnp.einsum("gmrd,mdk->gmrk", delta_sq, basis_sq, precision=highest)
    new_resid_sq = delta_sq - jnp.einsum("gmrk,mdk->gmrd", factor_sq, basis_sq, precision=highest)
    delta_up = start_up[None] - trained_up + resid_up
    factor_up = jnp.einsum("grf,fk->grk", delta_up, basis_up, precision=highest)
    new_resid_up = delta_up - jnp.einsum("grk,fk->grf", factor_up, basis_up, precision=highest)
    delta_down = start_down[None] - trained_down + resid_down
    factor_down = jnp.einsum("grd,dk->grk", delta_down, basis_down, precision=highest)
    new_resid_down = delta_down - jnp.einsum("grk,dk->grd", factor_down, basis_down, precision=highest)
    mean_sq = jnp.sum(factor_sq, axis=0) / GROUPS
    mean_up = jnp.sum(factor_up, axis=0) / GROUPS
    mean_down = jnp.sum(factor_down, axis=0) / GROUPS
    mean_ln = jnp.sum(start_ln[None] - trained_ln, axis=0) / GROUPS
    outer_sq = jnp.einsum("mrk,mdk->mrd", mean_sq, basis_sq, precision=highest)
    outer_up = jnp.einsum("rk,fk->rf", mean_up, basis_up, precision=highest)
    outer_down = jnp.einsum("rk,dk->rd", mean_down, basis_down, precision=highest)
    new_mom_sq, weights_sq = advance(start_sq, mom_sq, outer_sq)
    new_mom_up, weights_up = advance(start_up, mom_up, outer_up)
    new_mom_down, weights_down = advance(start_down, mom_down, outer_down)
    new_mom_ln, weights_ln = advance(start_ln, mom_ln, mean_ln)
    return (new_resid_sq, new_resid_up, new_resid_down, new_mom_sq, new_mom_up, new_mom_down, new_mom_ln, weights_sq, weights_up, weights_down, weights_ln)
```

```python
import functools

import jax
import jax.numpy as jnp
from jax import lax
from jax.experimental import pallas as pl
from jax.experimental.pallas import tpu as pltpu
from jax.sharding import PartitionSpec as P

moment_coef = 0.9
outer_rate = 0.7
MESH = pl.DeviceIdType.MESH
ANY = pl.BlockSpec(memory_space=pl.ANY)
VMEM = pl.BlockSpec(memory_space=pltpu.VMEM)
LANES = 128


def advance(start, moment, outer):
    new_moment = moment_coef * moment + outer
    weights = (start - outer_rate * (outer + moment_coef * new_moment)).astype(jnp.bfloat16)
    return (new_moment, weights)


def mean_kernel(groups, part_ref, mean_ref, landed, out_sem, in_sem, share_sem, got_sem):
    me, column = lax.axis_index("rep"), lax.axis_index("shard")
    barrier = pltpu.get_barrier_semaphore()
    peers = [lax.rem(me + step, groups) for step in range(1, groups)]
    for peer in peers:
        pl.semaphore_signal(barrier, inc=1, device_id=(peer, column), device_id_type=MESH)
    pl.semaphore_wait(barrier, groups - 1)
    scatter = [
        pltpu.make_async_remote_copy(
            part_ref.at[peer], landed.at[i], out_sem.at[i], in_sem.at[i],
            device_id=(peer, column), device_id_type=MESH,
        )
        for i, peer in enumerate(peers)
    ]
    for copy in scatter:
        copy.start()
    total = part_ref[me]
    for i, copy in enumerate(scatter):
        copy.wait_recv()
        total = total + landed[i]
    mean_ref[me] = total / groups
    share = [
        pltpu.make_async_remote_copy(
            mean_ref.at[me], mean_ref.at[me], share_sem.at[i], got_sem.at[i],
            device_id=(peer, column), device_id_type=MESH,
        )
        for i, peer in enumerate(peers)
    ]
    for copy in share:
        copy.start()
    for copy in scatter:
        copy.wait_send()
    for copy in share:
        copy.wait()


def mean_over_groups(part, groups):
    return pl.pallas_call(
        functools.partial(mean_kernel, groups),
        out_shape=jax.ShapeDtypeStruct(part.shape, part.dtype),
        in_specs=[VMEM],
        out_specs=VMEM,
        scratch_shapes=[pltpu.VMEM((groups - 1,) + part.shape[1:], part.dtype)]
        + [pltpu.SemaphoreType.DMA((groups - 1,))] * 4,
        compiler_params=pltpu.CompilerParams(collective_id=0, has_side_effects=True),
        name="mean_over_groups",
    )(part)


CHUNKS = 6


def gather_kernel(
    o_sq, o_up, o_dn, o_ln, w_sq, w_up, w_dn, w_ln,
    x_in, y_in, z_in, link_out, core_in, core_out, own_sem, ln_in, ln_out,
):
    plane, me = lax.axis_index("rep"), lax.axis_index("shard")
    parity = lax.rem(plane, 2)
    twin = plane + 1 - 2 * parity
    flip = lambda s, bit: s + bit - 2 * bit * lax.rem(s // bit, 2)
    side, across, sibling = flip(me, 2), flip(me, 4), flip(me, 1)
    corner = flip(side, 4)
    a, b = parity, 1 - parity

    barrier = pltpu.get_barrier_semaphore()
    mates = [lax.rem(me + step, 8) for step in range(1, 8)]
    for mate in mates:
        pl.semaphore_signal(barrier, inc=1, device_id=(plane, mate), device_id_type=MESH)
    pl.semaphore_signal(barrier, inc=1, device_id=(twin, me), device_id_type=MESH)
    pl.semaphore_wait(barrier, 8)

    rows = o_sq.shape[1]
    half = rows // 2
    width = o_sq.shape[2]
    deep = o_dn.shape[0]

    def piece(refs, owner, group, part, k):
        sq, up, dn = refs
        if k < 2:
            return sq.at[2 * group + k, pl.ds(pl.multiple_of(owner * rows + part * half, 16), half), :]
        if k < 4:
            return up.at[
                pl.ds(pl.multiple_of(owner * rows + part * half, 16), half),
                pl.ds(pl.multiple_of((2 * group + k - 2) * width, 128), width),
            ]
        return dn.at[
            pl.ds(pl.multiple_of(owner * deep + (4 * group + 2 * part + k - 4) * half, 16), half), :
        ]

    own, out = (o_sq, o_up, o_dn), (w_sq, w_up, w_dn)
    X, Y, Z = 0, 1, 2
    target = {X: (plane, side), Y: (plane, across), Z: (twin, me)}
    arrivals = {X: x_in, Y: y_in, Z: z_in}

    def send(way, kind, owner, group, part, k, mine=False):
        pltpu.make_async_remote_copy(
            piece(own, 0, group, part, k) if mine else piece(out, owner, group, part, k),
            piece(out, owner, group, part, k),
            link_out.at[way * 3 + k // 2],
            arrivals[way].at[kind * CHUNKS + k],
            device_id=target[way], device_id_type=MESH,
        ).start()

    def arrive(way, kind, owner, group, part, k):
        there = piece(out, owner, group, part, k)
        pltpu.make_async_copy(there, there, arrivals[way].at[kind * CHUNKS + k]).wait()
        pltpu.make_async_remote_copy(
            there, there, core_out.at[k // 2], core_in.at[k // 2],
            device_id=(plane, sibling), device_id_type=MESH,
        ).start()

    def first(k):
        send(X, 0, me, b, 0, k, True)
        send(Y, 0, me, b, 1, k, True)
        send(X, 1, me, a, 1, k, True)
        send(Y, 1, me, a, 0, k, True)

    def second(k):
        send(X, 3, me, a, 0, k, True)
        send(Y, 3, me, a, 1, k, True)

    first(0)
    second(0)
    first(1)

    homes = (
        w_sq.at[:, pl.ds(pl.multiple_of(me * rows, 16), rows), :],
        w_up.at[pl.ds(pl.multiple_of(me * rows, 16), rows), :],
        w_dn.at[pl.ds(pl.multiple_of(me * deep, 16), deep), :],
    )
    kept = [pltpu.make_async_copy(own[i], homes[i], own_sem.at[i]) for i in range(3)]
    kept.append(pltpu.make_async_copy(o_ln, w_ln.at[me], own_sem.at[3]))
    for copy in kept:
        copy.start()
    for i in range(3):
        pltpu.make_async_remote_copy(
            own[i], homes[i], core_out.at[i], core_in.at[i],
            device_id=(plane, sibling), device_id_type=MESH,
        ).start()
    norms = [
        pltpu.make_async_remote_copy(
            o_ln, w_ln.at[me], ln_out.at[i], ln_in.at[i],
            device_id=(plane, mate), device_id_type=MESH,
        )
        for i, mate in enumerate(mates)
    ]
    for copy in norms:
        copy.start()

    for k in range(CHUNKS + 2):
        if k < CHUNKS:
            arrive(X, 0, side, b, 0, k)
            send(Y, 2, side, b, 0, k)
            arrive(Y, 0, across, b, 1, k)
            send(X, 2, across, b, 1, k)
            arrive(X, 1, side, a, 1, k)
            send(Z, 2, side, a, 1, k)
            arrive(Y, 1, across, a, 0, k)
            send(Z, 3, across, a, 0, k)
            if k + 1 < CHUNKS:
                second(k + 1)
            if k + 2 < CHUNKS:
                first(k + 2)
        if 1 <= k <= CHUNKS:
            j = k - 1
            arrive(Y, 2, corner, b, 0, j)
            send(Z, 0, corner, b, 0, j)
            arrive(X, 2, corner, b, 1, j)
            send(Z, 1, corner, b, 1, j)
            arrive(X, 3, side, a, 0, j)
            arrive(Y, 3, across, a, 1, j)
        if k >= 2:
            j = k - 2
            arrive(Z, 2, side, b, 1, j)
            arrive(Z, 3, across, b, 0, j)
            arrive(Z, 0, corner, a, 0, j)
            arrive(Z, 1, corner, a, 1, j)

    for i in range(3):
        for way in range(3):
            pltpu.make_async_copy(own[i], own[i], link_out.at[way * 3 + i]).wait()
        share = (w_sq.at[:, pl.ds(0, 4 * rows), :], w_up.at[pl.ds(0, 4 * rows), :], w_dn.at[pl.ds(0, 4 * deep), :])[i]
        pltpu.make_async_copy(share, share, core_out.at[i]).wait()
        pltpu.make_async_copy(share, share, core_in.at[i]).wait()
    for copy in kept:
        copy.wait()
    for copy in norms:
        copy.wait()


def gather_weights(owned_sq, owned_up, owned_down, norm_weights, n):
    m, r, d = owned_sq.shape
    bf16 = jnp.bfloat16
    ln = jnp.pad(norm_weights, ((0, 16 - norm_weights.shape[0]), (0, LANES - norm_weights.shape[1])))
    dma = pltpu.SemaphoreType.DMA
    sq, up, down, lns = pl.pallas_call(
        gather_kernel,
        out_shape=[
            jax.ShapeDtypeStruct((m, n * r, d), bf16),
            jax.ShapeDtypeStruct((n * owned_up.shape[0], owned_up.shape[1]), bf16),
            jax.ShapeDtypeStruct((n * owned_down.shape[0], owned_down.shape[1]), bf16),
            jax.ShapeDtypeStruct((n,) + ln.shape, bf16),
        ],
        in_specs=[ANY] * 4,
        out_specs=[ANY] * 4,
        scratch_shapes=[
            dma((4 * CHUNKS,)), dma((4 * CHUNKS,)), dma((4 * CHUNKS,)),
            dma((9,)), dma((3,)), dma((3,)), dma((4,)), dma((7,)), dma((7,)),
        ],
        compiler_params=pltpu.CompilerParams(collective_id=1, has_side_effects=True),
        name="gather_weights",
    )(owned_sq, owned_up, owned_down, ln)
    lns = lns[:, : norm_weights.shape[0], : norm_weights.shape[1]]
    return sq, up, down, lns.transpose(1, 0, 2).reshape(norm_weights.shape[0], -1)


def on_device(
    trained_sq,
    trained_up,
    trained_down,
    trained_ln,
    start_sq,
    start_up,
    start_down,
    start_ln,
    resid_sq,
    resid_up,
    resid_down,
    mom_sq,
    mom_up,
    mom_down,
    mom_ln,
    basis_sq,
    basis_up,
    basis_down,
):
    fine = lax.Precision.HIGH
    groups = lax.axis_size("rep")
    shards = lax.axis_size("shard")
    delta_sq = start_sq - trained_sq[0] + resid_sq[0]
    factor_sq = jnp.einsum("mrd,mdk->mrk", delta_sq, basis_sq, precision=fine)
    delta_up = start_up - trained_up[0] + resid_up[0]
    factor_up = jnp.dot(delta_up, basis_up, precision=fine, preferred_element_type=jnp.float32)
    delta_down = start_down - trained_down[0] + resid_down[0]
    factor_down = jnp.dot(delta_down, basis_down, precision=fine, preferred_element_type=jnp.float32)
    norm_delta = start_ln - trained_ln[0]

    parts = (factor_sq, factor_up, factor_down, norm_delta)
    flat = jnp.concatenate([part.reshape(-1) for part in parts])
    slot = -(-flat.size // (groups * 8 * LANES)) * 8
    flat = jnp.pad(flat, (0, groups * slot * LANES - flat.size))
    mean = mean_over_groups(flat.reshape(groups, slot, LANES), groups).reshape(-1)
    means, at = [], 0
    for part in parts:
        means.append(mean[at : at + part.size].reshape(part.shape))
        at += part.size
    mean_sq, mean_up, mean_down, mean_ln = means

    new_resid_sq = delta_sq - jnp.einsum("mrk,mdk->mrd", factor_sq, basis_sq, precision=fine)
    new_resid_up = delta_up - jnp.einsum("rk,fk->rf", factor_up, basis_up, precision=fine)
    new_resid_down = delta_down - jnp.einsum("rk,dk->rd", factor_down, basis_down, precision=fine)
    new_mom_ln, norm_weights = advance(start_ln, mom_ln, mean_ln)
    outer_sq = jnp.einsum("mrk,mdk->mrd", mean_sq, basis_sq, precision=fine)
    outer_up = jnp.einsum("rk,fk->rf", mean_up, basis_up, precision=fine)
    outer_down = jnp.einsum("rk,dk->rd", mean_down, basis_down, precision=fine)
    new_mom_sq, owned_sq = advance(start_sq, mom_sq, outer_sq)
    new_mom_up, owned_up = advance(start_up, mom_up, outer_up)
    new_mom_down, owned_down = advance(start_down, mom_down, outer_down)
    if shards == 8 and groups % 2 == 0:
        weights = gather_weights(owned_sq, owned_up, owned_down, norm_weights, shards)
    else:
        weights = (
            lax.all_gather(owned_sq, "shard", axis=1, tiled=True),
            lax.all_gather(owned_up, "shard", axis=0, tiled=True),
            lax.all_gather(owned_down, "shard", axis=0, tiled=True),
            lax.all_gather(norm_weights, "shard", axis=1, tiled=True),
        )
    return (
        new_resid_sq[None],
        new_resid_up[None],
        new_resid_down[None],
        new_mom_sq,
        new_mom_up,
        new_mom_down,
        new_mom_ln,
        *weights,
    )


def solution(mesh):
    placed = (
        P("rep", None, "shard", None),
        P("rep", "shard", None),
        P("rep", "shard", None),
        P("rep", None, "shard"),
        P(None, "shard", None),
        P("shard", None),
        P("shard", None),
        P(None, "shard"),
        P("rep", None, "shard", None),
        P("rep", "shard", None),
        P("rep", "shard", None),
        P(None, "shard", None),
        P("shard", None),
        P("shard", None),
        P(None, "shard"),
        P(),
        P(),
        P(),
    )
    return jax.shard_map(
        on_device,
        mesh=mesh,
        in_specs=placed,
        out_specs=(
            P("rep", None, "shard", None),
            P("rep", "shard", None),
            P("rep", "shard", None),
            P(None, "shard", None),
            P("shard", None),
            P("shard", None),
            P(None, "shard"),
            P(),
            P(),
            P(),
            P(),
        ),
        check_vma=False,
    )
```

```python
import functools

import jax
import jax.numpy as jnp
from jax import lax
from jax.experimental import pallas as pl
from jax.experimental.pallas import tpu as pltpu
from jax.sharding import PartitionSpec as P

moment_coef = 0.9
outer_rate = 0.7
MESH = pl.DeviceIdType.MESH
ANY = pl.BlockSpec(memory_space=pl.ANY)
VMEM = pl.BlockSpec(memory_space=pltpu.VMEM)
LANES = 128


def advance(start, moment, outer):
    new_moment = moment_coef * moment + outer
    weights = (start - outer_rate * (outer + moment_coef * new_moment)).astype(jnp.bfloat16)
    return (new_moment, weights)


def mean_kernel(groups, part_ref, mean_ref, landed, out_sem, in_sem, share_sem, got_sem):
    me, column = lax.axis_index("rep"), lax.axis_index("shard")
    barrier = pltpu.get_barrier_semaphore()
    peers = [lax.rem(me + step, groups) for step in range(1, groups)]
    for peer in peers:
        pl.semaphore_signal(barrier, inc=1, device_id=(peer, column), device_id_type=MESH)
    pl.semaphore_wait(barrier, groups - 1)
    scatter = [
        pltpu.make_async_remote_copy(
            part_ref.at[peer], landed.at[i], out_sem.at[i], in_sem.at[i],
            device_id=(peer, column), device_id_type=MESH,
        )
        for i, peer in enumerate(peers)
    ]
    for copy in scatter:
        copy.start()
    total = part_ref[me]
    for i, copy in enumerate(scatter):
        copy.wait_recv()
        total = total + landed[i]
    mean_ref[me] = total / groups
    share = [
        pltpu.make_async_remote_copy(
            mean_ref.at[me], mean_ref.at[me], share_sem.at[i], got_sem.at[i],
            device_id=(peer, column), device_id_type=MESH,
        )
        for i, peer in enumerate(peers)
    ]
    for copy in share:
        copy.start()
    for copy in scatter:
        copy.wait_send()
    for copy in share:
        copy.wait()


def mean_over_groups(part, groups):
    return pl.pallas_call(
        functools.partial(mean_kernel, groups),
        out_shape=jax.ShapeDtypeStruct(part.shape, part.dtype),
        in_specs=[VMEM],
        out_specs=VMEM,
        scratch_shapes=[pltpu.VMEM((groups - 1,) + part.shape[1:], part.dtype)]
        + [pltpu.SemaphoreType.DMA((groups - 1,))] * 4,
        compiler_params=pltpu.CompilerParams(collective_id=0, has_side_effects=True),
        name="mean_over_groups",
    )(part)


CHUNKS = 6


def halves(x):
    top = x.astype(jnp.bfloat16)
    return top, (x - top.astype(jnp.float32)).astype(jnp.bfloat16)


def times(x, top, low, dims):
    x_top, x_low = halves(x)
    dot = lambda u, v: lax.dot_general(u, v, (dims, ((), ())), preferred_element_type=jnp.float32)
    return dot(x_top, top) + (dot(x_top, low) + dot(x_low, top))


def step_kernel(
    t_sq, t_up, t_dn, s_sq, s_up, s_dn, r_sq, r_up, r_dn, m_sq, m_up, m_dn,
    t_ln, s_ln, m_ln, basis_sq, basis_up, basis_dn,
    nr_sq, nr_up, nr_dn, nm_sq, nm_up, nm_dn, nm_ln, w_sq, w_up, w_dn, w_ln,
    vt_sq, vt_up, vt_dn, vs_sq, vs_up, vs_dn, vr_sq, vr_up, vr_dn, vm_sq, vm_up, vm_dn,
    o_sq, o_up, o_dn, o_ln, wide, top, low, part, mean, landed,
    load_sem, store_sem, out_sem, in_sem, share_sem, got_sem,
    x_in, y_in, z_in, link_out, core_in, core_out, own_sem, ln_in, ln_out,
):
    groups = 4
    plane, me = lax.axis_index("rep"), lax.axis_index("shard")
    parity = lax.rem(plane, 2)
    twin = plane + 1 - 2 * parity
    flip = lambda s, bit: s + bit - 2 * bit * lax.rem(s // bit, 2)
    side, across, sibling = flip(me, 2), flip(me, 4), flip(me, 1)
    corner = flip(side, 4)
    a, b = parity, 1 - parity

    barrier = pltpu.get_barrier_semaphore()
    mates = [lax.rem(me + step, 8) for step in range(1, 8)]
    peers = [lax.rem(plane + step, groups) for step in range(1, groups)]
    for mate in mates:
        pl.semaphore_signal(barrier, inc=1, device_id=(plane, mate), device_id_type=MESH)
    for peer in peers:
        pl.semaphore_signal(barrier, inc=1, device_id=(peer, me), device_id_type=MESH)

    loads = [
        pltpu.make_async_copy(src, dst, load_sem.at[i])
        for i, (src, dst) in enumerate([
            (t_sq, vt_sq), (s_sq, vs_sq), (r_sq, vr_sq),
            (t_dn, vt_dn), (s_dn, vs_dn), (r_dn, vr_dn),
            (t_up, vt_up), (s_up, vs_up), (r_up, vr_up),
            (m_sq, vm_sq), (m_up, vm_up), (m_dn, vm_dn),
        ])
    ]
    for copy in loads:
        copy.start()

    rows, width = vs_sq.shape[1], vs_sq.shape[2]
    half, deep, rank = rows // 2, vs_dn.shape[0], basis_dn.shape[1]
    DN, UP = 4 * width, 6 * width
    wide[...] = jnp.zeros_like(wide)

    def lay(block, *places):
        wide[:, :rank] = block
        x = wide[...]
        for place, high in places:
            top[pl.ds(place, width), :], low[pl.ds(place, width), :] = halves(pltpu.roll(x, rank, 1) if high else x)

    for m in range(4):
        lay(basis_sq[m], (m * width, m % 2))
    lay(basis_dn[...], (DN, 0), (DN + width, 1))
    for c in range(4):
        lay(basis_up[pl.ds(c * width, width), :], (UP + c * width, 0), (UP + (4 + c) * width, 1))

    def factor(delta, place):
        return times(delta, top[pl.ds(place, width), :], low[pl.ds(place, width), :], ((1,), (0,)))

    for i in range(3):
        loads[i].wait()
    for pair in range(2):
        total = None
        for m in (2 * pair, 2 * pair + 1):
            delta = vs_sq[m] - vt_sq[m] + vr_sq[m]
            vr_sq[m] = delta
            f = factor(delta, m * width)
            total = f if total is None else total + f
        part[pl.ds(pair * rows, rows), :] = total
    for i in range(3, 6):
        loads[i].wait()
    for g in range(2):
        total = None
        for high in range(2):
            at = pl.ds(high * (deep // 2) + g * rows, rows)
            delta = vs_dn[at, :] - vt_dn[at, :] + vr_dn[at, :]
            vr_dn[at, :] = delta
            f = factor(delta, DN + high * width)
            total = f if total is None else total + f
        part[pl.ds(2 * rows + g * rows, rows), :] = total
    for i in range(6, 9):
        loads[i].wait()
    total = None
    for high in range(2):
        for c in range(4):
            at = (pl.ds(high * half, half), pl.ds(c * width, width))
            delta = vs_up[at] - vt_up[at] + vr_up[at]
            vr_up[at] = delta
            f = factor(delta, UP + (4 * high + c) * width)
            total = f if total is None else total + f
    part[pl.ds(4 * rows, half), :] = total
    tail = 4 * rows + half
    part[pl.ds(tail, 16), :] = jnp.zeros((16, LANES), jnp.float32)
    part[pl.ds(tail, 4), :rows] = s_ln[...] - t_ln[...]

    pl.semaphore_wait(barrier, 10)
    slot = part.shape[0] // groups
    rows_of = lambda g: pl.ds(pl.multiple_of(g * slot, 8), slot)
    scatter = [
        pltpu.make_async_remote_copy(
            part.at[rows_of(peer), :], landed.at[i], out_sem.at[i], in_sem.at[i],
            device_id=(peer, me), device_id_type=MESH,
        )
        for i, peer in enumerate(peers)
    ]
    for copy in scatter:
        copy.start()
    total = part[rows_of(plane), :]
    for i, copy in enumerate(scatter):
        copy.wait_recv()
        total = total + landed[i]
    mean[rows_of(plane), :] = total / groups
    share = [
        pltpu.make_async_remote_copy(
            mean.at[rows_of(plane), :], mean.at[rows_of(plane), :], share_sem.at[i], got_sem.at[i],
            device_id=(peer, me), device_id_type=MESH,
        )
        for i, peer in enumerate(peers)
    ]
    for copy in share:
        copy.start()
    for i in range(9, 12):
        loads[i].wait()
    for copy in scatter:
        copy.wait_send()
    for copy in share:
        copy.wait()

    def piece(refs, owner, group, part_, k):
        sq, up, dn = refs
        if k < 2:
            return sq.at[2 * group + k, pl.ds(pl.multiple_of(owner * rows + part_ * half, 16), half), :]
        if k < 4:
            return up.at[
                pl.ds(pl.multiple_of(owner * rows + part_ * half, 16), half),
                pl.ds(pl.multiple_of((2 * group + k - 2) * width, 128), width),
            ]
        return dn.at[
            pl.ds(pl.multiple_of(owner * deep + (4 * group + 2 * part_ + k - 4) * half, 16), half), :
        ]

    def places(group, h, k):
        if k < 2:
            return group * rows + h * half, (2 * group + k) * width
        if k < 4:
            return 4 * rows, UP + (4 * h + 2 * group + k - 2) * width
        return 2 * rows + (2 * h + k - 4) * half, DN + group * width

    def spread(ref, group, h, k):
        row, place = places(group, h, k)
        row = row if isinstance(row, int) else pl.multiple_of(row, 16)
        at = pl.ds(pl.multiple_of(place, 16), width)
        return times(ref[pl.ds(row, half), :], top[at, :], low[at, :], ((1,), (1,)))

    vs, vr, vm = (vs_sq, vs_up, vs_dn), (vr_sq, vr_up, vr_dn), (vm_sq, vm_up, vm_dn)
    own, out = (o_sq, o_up, o_dn), (w_sq, w_up, w_dn)

    def update(group, h, k):
        outer = spread(mean, group, h, k)
        moment = piece(vm, 0, group, h, k)
        new_moment, weights = advance(piece(vs, 0, group, h, k)[...], moment[...], outer)
        moment[...] = new_moment
        piece(own, 0, group, h, k)[...] = weights

    def leave(group, h, k):
        delta = piece(vr, 0, group, h, k)
        delta[...] = delta[...] - spread(part, group, h, k)

    X, Y, Z = 0, 1, 2
    target = {X: (plane, side), Y: (plane, across), Z: (twin, me)}
    arrivals = {X: x_in, Y: y_in, Z: z_in}

    def send(way, kind, owner, group, h, k, mine=False):
        pltpu.make_async_remote_copy(
            piece(own, 0, group, h, k) if mine else piece(out, owner, group, h, k),
            piece(out, owner, group, h, k),
            link_out.at[way * 3 + k // 2],
            arrivals[way].at[kind * CHUNKS + k],
            device_id=target[way], device_id_type=MESH,
        ).start()

    def arrive(way, kind, owner, group, h, k):
        there = piece(out, owner, group, h, k)
        pltpu.make_async_copy(there, there, arrivals[way].at[kind * CHUNKS + k]).wait()
        pltpu.make_async_remote_copy(
            there, there, core_out.at[k // 2], core_in.at[k // 2],
            device_id=(plane, sibling), device_id_type=MESH,
        ).start()

    def first(k):
        update(b, 0, k)
        send(X, 0, me, b, 0, k, True)
        update(b, 1, k)
        send(Y, 0, me, b, 1, k, True)
        update(a, 1, k)
        send(X, 1, me, a, 1, k, True)
        update(a, 0, k)
        send(Y, 1, me, a, 0, k, True)

    def second(k):
        send(X, 3, me, a, 0, k, True)
        send(Y, 3, me, a, 1, k, True)

    for k in range(3):
        first(k)
    nm_value, ln_value = advance(s_ln[...], m_ln[...], mean[pl.ds(tail, 4), :][:, :rows])
    nm_ln[...] = nm_value
    o_ln[...] = jnp.zeros_like(o_ln)
    o_ln[:4, :rows] = ln_value
    norms = [
        pltpu.make_async_remote_copy(
            o_ln, w_ln.at[me], ln_out.at[i], ln_in.at[i],
            device_id=(plane, mate), device_id_type=MESH,
        )
        for i, mate in enumerate(mates)
    ]
    for copy in norms:
        copy.start()

    homes = (
        w_sq.at[:, pl.ds(pl.multiple_of(me * rows, 16), rows), :],
        w_up.at[pl.ds(pl.multiple_of(me * rows, 16), rows), :],
        w_dn.at[pl.ds(pl.multiple_of(me * deep, 16), deep), :],
    )
    kept = [pltpu.make_async_copy(own[i], homes[i], own_sem.at[i]) for i in range(3)]
    kept.append(pltpu.make_async_copy(o_ln, w_ln.at[me], own_sem.at[3]))
    stores = [
        pltpu.make_async_copy(src, dst, store_sem.at[i])
        for i, (src, dst) in enumerate([
            (vm_sq, nm_sq), (vm_up, nm_up), (vm_dn, nm_dn), (vr_sq, nr_sq), (vr_up, nr_up), (vr_dn, nr_dn),
        ])
    ]

    for k in range(CHUNKS + 2):
        if k < CHUNKS:
            arrive(X, 0, side, b, 0, k)
            send(Y, 2, side, b, 0, k)
            arrive(Y, 0, across, b, 1, k)
            send(X, 2, across, b, 1, k)
            arrive(X, 1, side, a, 1, k)
            send(Z, 2, side, a, 1, k)
            arrive(Y, 1, across, a, 0, k)
            send(Z, 3, across, a, 0, k)
        if 1 <= k <= CHUNKS:
            j = k - 1
            arrive(Y, 2, corner, b, 0, j)
            send(Z, 0, corner, b, 0, j)
            arrive(X, 2, corner, b, 1, j)
            send(Z, 1, corner, b, 1, j)
        if k + 3 < CHUNKS:
            first(k + 3)
        for j in {3: (0,), 4: (1, 2), 5: (3, 4, 5)}.get(k, ()):
            second(j)
        if k == 3:
            for i in range(3):
                kept[i].start()
                stores[i].start()
                pltpu.make_async_remote_copy(
                    own[i], homes[i], core_out.at[i], core_in.at[i],
                    device_id=(plane, sibling), device_id_type=MESH,
                ).start()
            kept[3].start()
        if k < CHUNKS:
            for group in range(2):
                for h in range(2):
                    leave(group, h, k)
            if k % 2:
                stores[3 + k // 2].start()

    for j in range(CHUNKS):
        arrive(Z, 2, side, b, 1, j)
        arrive(Z, 3, across, b, 0, j)
        arrive(Z, 0, corner, a, 0, j)
        arrive(Z, 1, corner, a, 1, j)
        arrive(X, 3, side, a, 0, j)
        arrive(Y, 3, across, a, 1, j)

    for i in range(3):
        for way in range(3):
            pltpu.make_async_copy(own[i], own[i], link_out.at[way * 3 + i]).wait()
        share_ = (w_sq.at[:, pl.ds(0, 4 * rows), :], w_up.at[pl.ds(0, 4 * rows), :], w_dn.at[pl.ds(0, 4 * deep), :])[i]
        pltpu.make_async_copy(share_, share_, core_out.at[i]).wait()
        pltpu.make_async_copy(share_, share_, core_in.at[i]).wait()
    for copy in kept + norms + stores:
        copy.wait()


def whole_step(trained, start, resid, moment, norms, bases, n):
    f32, bf16, dma = jnp.float32, jnp.bfloat16, pltpu.SemaphoreType.DMA
    shape = jax.ShapeDtypeStruct
    sq, up, dn = (x.shape for x in start)
    tall = 14 * sq[2]
    held = [pltpu.VMEM(x, f32) for x in (sq, up, dn)]
    results = pl.pallas_call(
        step_kernel,
        out_shape=[shape(x, f32) for x in (sq, up, dn, sq, up, dn, norms[0].shape)]
        + [
            shape((sq[0], n * sq[1], sq[2]), bf16),
            shape((n * up[0], up[1]), bf16),
            shape((n * dn[0], dn[1]), bf16),
            shape((n, 16, LANES), bf16),
        ],
        in_specs=[ANY] * 12 + [VMEM] * 6,
        out_specs=[ANY] * 6 + [VMEM] + [ANY] * 4,
        scratch_shapes=held * 4
        + [pltpu.VMEM(x, bf16) for x in (sq, up, dn, (16, LANES))]
        + [pltpu.VMEM((sq[2], LANES), f32), pltpu.VMEM((tall, LANES), bf16), pltpu.VMEM((tall, LANES), bf16)]
        + [pltpu.VMEM((448, LANES), f32), pltpu.VMEM((448, LANES), f32), pltpu.VMEM((3, 112, LANES), f32)]
        + [dma((12,)), dma((6,)), dma((3,)), dma((3,)), dma((3,)), dma((3,))]
        + [dma((4 * CHUNKS,))] * 3
        + [dma((9,)), dma((3,)), dma((3,)), dma((4,)), dma((7,)), dma((7,))],
        compiler_params=pltpu.CompilerParams(
            collective_id=1, has_side_effects=True, vmem_limit_bytes=56 * 2**20
        ),
        name="whole_step",
    )(*trained, *start, *resid, *moment, *norms, *bases)
    *rest, lns = results
    lns = lns[:, : norms[0].shape[0], : norms[0].shape[1]].transpose(1, 0, 2).reshape(norms[0].shape[0], -1)
    nr = [x[None] for x in rest[:3]]
    return (*nr, *rest[3:], lns)


def on_device(
    trained_sq,
    trained_up,
    trained_down,
    trained_ln,
    start_sq,
    start_up,
    start_down,
    start_ln,
    resid_sq,
    resid_up,
    resid_down,
    mom_sq,
    mom_up,
    mom_down,
    mom_ln,
    basis_sq,
    basis_up,
    basis_down,
):
    fine = lax.Precision.HIGH
    groups = lax.axis_size("rep")
    shards = lax.axis_size("shard")
    if shards == 8 and groups == 4 and basis_down.shape[1] * 2 == LANES:
        return whole_step(
            (trained_sq[0], trained_up[0], trained_down[0]),
            (start_sq, start_up, start_down),
            (resid_sq[0], resid_up[0], resid_down[0]),
            (mom_sq, mom_up, mom_down),
            (trained_ln[0], start_ln, mom_ln),
            (basis_sq, basis_up, basis_down),
            shards,
        )
    delta_sq = start_sq - trained_sq[0] + resid_sq[0]
    factor_sq = jnp.einsum("mrd,mdk->mrk", delta_sq, basis_sq, precision=fine)
    delta_up = start_up - trained_up[0] + resid_up[0]
    factor_up = jnp.dot(delta_up, basis_up, precision=fine, preferred_element_type=jnp.float32)
    delta_down = start_down - trained_down[0] + resid_down[0]
    factor_down = jnp.dot(delta_down, basis_down, precision=fine, preferred_element_type=jnp.float32)
    norm_delta = start_ln - trained_ln[0]

    parts = (factor_sq, factor_up, factor_down, norm_delta)
    flat = jnp.concatenate([part.reshape(-1) for part in parts])
    slot = -(-flat.size // (groups * 8 * LANES)) * 8
    flat = jnp.pad(flat, (0, groups * slot * LANES - flat.size))
    mean = mean_over_groups(flat.reshape(groups, slot, LANES), groups).reshape(-1)
    means, at = [], 0
    for part in parts:
        means.append(mean[at : at + part.size].reshape(part.shape))
        at += part.size
    mean_sq, mean_up, mean_down, mean_ln = means

    new_resid_sq = delta_sq - jnp.einsum("mrk,mdk->mrd", factor_sq, basis_sq, precision=fine)
    new_resid_up = delta_up - jnp.einsum("rk,fk->rf", factor_up, basis_up, precision=fine)
    new_resid_down = delta_down - jnp.einsum("rk,dk->rd", factor_down, basis_down, precision=fine)
    new_mom_ln, norm_weights = advance(start_ln, mom_ln, mean_ln)
    outer_sq = jnp.einsum("mrk,mdk->mrd", mean_sq, basis_sq, precision=fine)
    outer_up = jnp.einsum("rk,fk->rf", mean_up, basis_up, precision=fine)
    outer_down = jnp.einsum("rk,dk->rd", mean_down, basis_down, precision=fine)
    new_mom_sq, owned_sq = advance(start_sq, mom_sq, outer_sq)
    new_mom_up, owned_up = advance(start_up, mom_up, outer_up)
    new_mom_down, owned_down = advance(start_down, mom_down, outer_down)
    weights = (
        lax.all_gather(owned_sq, "shard", axis=1, tiled=True),
        lax.all_gather(owned_up, "shard", axis=0, tiled=True),
        lax.all_gather(owned_down, "shard", axis=0, tiled=True),
        lax.all_gather(norm_weights, "shard", axis=1, tiled=True),
    )
    return (
        new_resid_sq[None],
        new_resid_up[None],
        new_resid_down[None],
        new_mom_sq,
        new_mom_up,
        new_mom_down,
        new_mom_ln,
        *weights,
    )


def solution(mesh):
    placed = (
        P("rep", None, "shard", None),
        P("rep", "shard", None),
        P("rep", "shard", None),
        P("rep", None, "shard"),
        P(None, "shard", None),
        P("shard", None),
        P("shard", None),
        P(None, "shard"),
        P("rep", None, "shard", None),
        P("rep", "shard", None),
        P("rep", "shard", None),
        P(None, "shard", None),
        P("shard", None),
        P("shard", None),
        P(None, "shard"),
        P(),
        P(),
        P(),
    )
    return jax.shard_map(
        on_device,
        mesh=mesh,
        in_specs=placed,
        out_specs=(
            P("rep", None, "shard", None),
            P("rep", "shard", None),
            P("rep", "shard", None),
            P(None, "shard", None),
            P("shard", None),
            P("shard", None),
            P(None, "shard"),
            P(),
            P(),
            P(),
            P(),
        ),
        check_vma=False,
    )
```

```python
import functools

import jax
import jax.numpy as jnp
from jax import lax
from jax.experimental import pallas as pl
from jax.experimental.pallas import tpu as pltpu
from jax.sharding import PartitionSpec as P

moment_coef = 0.9
outer_rate = 0.7
MESH = pl.DeviceIdType.MESH
ANY = pl.BlockSpec(memory_space=pl.ANY)
VMEM = pl.BlockSpec(memory_space=pltpu.VMEM)
LANES = 128


def advance(start, moment, outer):
    new_moment = moment_coef * moment + outer
    weights = (start - outer_rate * (outer + moment_coef * new_moment)).astype(jnp.bfloat16)
    return (new_moment, weights)


def mean_kernel(groups, part_ref, mean_ref, landed, out_sem, in_sem, share_sem, got_sem):
    me, column = lax.axis_index("rep"), lax.axis_index("shard")
    barrier = pltpu.get_barrier_semaphore()
    peers = [lax.rem(me + step, groups) for step in range(1, groups)]
    for peer in peers:
        pl.semaphore_signal(barrier, inc=1, device_id=(peer, column), device_id_type=MESH)
    pl.semaphore_wait(barrier, groups - 1)
    scatter = [
        pltpu.make_async_remote_copy(
            part_ref.at[peer], landed.at[i], out_sem.at[i], in_sem.at[i],
            device_id=(peer, column), device_id_type=MESH,
        )
        for i, peer in enumerate(peers)
    ]
    for copy in scatter:
        copy.start()
    total = part_ref[me]
    for i, copy in enumerate(scatter):
        copy.wait_recv()
        total = total + landed[i]
    mean_ref[me] = total / groups
    share = [
        pltpu.make_async_remote_copy(
            mean_ref.at[me], mean_ref.at[me], share_sem.at[i], got_sem.at[i],
            device_id=(peer, column), device_id_type=MESH,
        )
        for i, peer in enumerate(peers)
    ]
    for copy in share:
        copy.start()
    for copy in scatter:
        copy.wait_send()
    for copy in share:
        copy.wait()


def mean_over_groups(part, groups):
    return pl.pallas_call(
        functools.partial(mean_kernel, groups),
        out_shape=jax.ShapeDtypeStruct(part.shape, part.dtype),
        in_specs=[VMEM],
        out_specs=VMEM,
        scratch_shapes=[pltpu.VMEM((groups - 1,) + part.shape[1:], part.dtype)]
        + [pltpu.SemaphoreType.DMA((groups - 1,))] * 4,
        compiler_params=pltpu.CompilerParams(collective_id=0, has_side_effects=True),
        name="mean_over_groups",
    )(part)


CHUNKS = 6


def halves(x):
    top = x.astype(jnp.bfloat16)
    return top, (x - top.astype(jnp.float32)).astype(jnp.bfloat16)


def times(x, top, low, dims):
    x_top, x_low = halves(x)
    dot = lambda u, v: lax.dot_general(u, v, (dims, ((), ())), preferred_element_type=jnp.float32)
    return dot(x_top, top) + (dot(x_top, low) + dot(x_low, top))


def step_kernel(
    t_sq, t_up, t_dn, s_sq, s_up, s_dn, r_sq, r_up, r_dn, m_sq, m_up, m_dn,
    t_ln, s_ln, m_ln, basis_sq, basis_up, basis_dn,
    nr_sq, nr_up, nr_dn, nm_sq, nm_up, nm_dn, nm_ln, w_sq, w_up, w_dn, w_ln,
    vt_sq, vt_up, vt_dn, vs_sq, vs_up, vs_dn, vr_sq, vr_up, vr_dn, vm_sq, vm_up, vm_dn,
    o_sq, o_up, o_dn, o_ln, wide, top, low, part, mean, landed,
    load_sem, store_sem, out_sem, in_sem, share_sem, got_sem,
    x_in, y_in, z_in, link_out, core_in, core_out, own_sem, ln_in, ln_out,
):
    groups = 4
    plane, me = lax.axis_index("rep"), lax.axis_index("shard")
    parity = lax.rem(plane, 2)
    twin = plane + 1 - 2 * parity
    flip = lambda s, bit: s + bit - 2 * bit * lax.rem(s // bit, 2)
    side, across, sibling = flip(me, 2), flip(me, 4), flip(me, 1)
    corner = flip(side, 4)
    a, b = parity, 1 - parity

    barrier = pltpu.get_barrier_semaphore()
    mates = [lax.rem(me + step, 8) for step in range(1, 8)]
    peers = [lax.rem(plane + step, groups) for step in range(1, groups)]
    for mate in mates:
        pl.semaphore_signal(barrier, inc=1, device_id=(plane, mate), device_id_type=MESH)
    for peer in peers:
        pl.semaphore_signal(barrier, inc=1, device_id=(peer, me), device_id_type=MESH)

    loads = [
        pltpu.make_async_copy(src, dst, load_sem.at[i])
        for i, (src, dst) in enumerate([
            (t_sq, vt_sq), (s_sq, vs_sq), (r_sq, vr_sq),
            (t_dn, vt_dn), (s_dn, vs_dn), (r_dn, vr_dn),
            (t_up, vt_up), (s_up, vs_up), (r_up, vr_up),
            (m_sq, vm_sq), (m_up, vm_up), (m_dn, vm_dn),
        ])
    ]
    for copy in loads:
        copy.start()

    rows, width = vs_sq.shape[1], vs_sq.shape[2]
    half, deep, rank = rows // 2, vs_dn.shape[0], basis_dn.shape[0]
    DN, UP = 4 * width, 6 * width
    wide[...] = jnp.zeros_like(wide)

    def lay(block, *places):
        wide[:, :rank] = block
        x = wide[...]
        for place, high in places:
            top[pl.ds(place, width), :], low[pl.ds(place, width), :] = halves(pltpu.roll(x, rank, 1) if high else x)

    for m in range(4):
        lay(basis_sq[m].T, (m * width, m % 2))
    lay(basis_dn[...].T, (DN, 0), (DN + width, 1))
    for c in range(4):
        lay(basis_up[:, pl.ds(c * width, width)].T, (UP + c * width, 0), (UP + (4 + c) * width, 1))

    def factor(delta, place):
        return times(delta, top[pl.ds(place, width), :], low[pl.ds(place, width), :], ((1,), (0,)))

    for i in range(3):
        loads[i].wait()
    for pair in range(2):
        total = None
        for m in (2 * pair, 2 * pair + 1):
            delta = vs_sq[m] - vt_sq[m] + vr_sq[m]
            vr_sq[m] = delta
            f = factor(delta, m * width)
            total = f if total is None else total + f
        part[pl.ds(pair * rows, rows), :] = total
    for i in range(3, 6):
        loads[i].wait()
    for g in range(2):
        total = None
        for high in range(2):
            at = pl.ds(high * (deep // 2) + g * rows, rows)
            delta = vs_dn[at, :] - vt_dn[at, :] + vr_dn[at, :]
            vr_dn[at, :] = delta
            f = factor(delta, DN + high * width)
            total = f if total is None else total + f
        part[pl.ds(2 * rows + g * rows, rows), :] = total
    for i in range(6, 9):
        loads[i].wait()
    total = None
    for high in range(2):
        for c in range(4):
            at = (pl.ds(high * half, half), pl.ds(c * width, width))
            delta = vs_up[at] - vt_up[at] + vr_up[at]
            vr_up[at] = delta
            f = factor(delta, UP + (4 * high + c) * width)
            total = f if total is None else total + f
    part[pl.ds(4 * rows, half), :] = total
    tail = 4 * rows + half
    part[pl.ds(tail, 16), :] = jnp.zeros((16, LANES), jnp.float32)
    part[pl.ds(tail, 4), :rows] = s_ln[...] - t_ln[...]

    pl.semaphore_wait(barrier, 10)
    slot = part.shape[0] // groups
    rows_of = lambda g: pl.ds(pl.multiple_of(g * slot, 8), slot)
    scatter = [
        pltpu.make_async_remote_copy(
            part.at[rows_of(peer), :], landed.at[i], out_sem.at[i], in_sem.at[i],
            device_id=(peer, me), device_id_type=MESH,
        )
        for i, peer in enumerate(peers)
    ]
    for copy in scatter:
        copy.start()
    total = part[rows_of(plane), :]
    for i, copy in enumerate(scatter):
        copy.wait_recv()
        total = total + landed[i]
    mean[rows_of(plane), :] = total / groups
    share = [
        pltpu.make_async_remote_copy(
            mean.at[rows_of(plane), :], mean.at[rows_of(plane), :], share_sem.at[i], got_sem.at[i],
            device_id=(peer, me), device_id_type=MESH,
        )
        for i, peer in enumerate(peers)
    ]
    for copy in share:
        copy.start()
    for i in range(9, 12):
        loads[i].wait()
    for copy in scatter:
        copy.wait_send()
    for copy in share:
        copy.wait()

    def piece(refs, owner, group, part_, k):
        sq, up, dn = refs
        if k < 2:
            return sq.at[2 * group + k, pl.ds(pl.multiple_of(owner * rows + part_ * half, 16), half), :]
        if k < 4:
            return up.at[
                pl.ds(pl.multiple_of(owner * rows + part_ * half, 16), half),
                pl.ds(pl.multiple_of((2 * group + k - 2) * width, 128), width),
            ]
        return dn.at[
            pl.ds(pl.multiple_of(owner * deep + (4 * group + 2 * part_ + k - 4) * half, 16), half), :
        ]

    def places(group, h, k):
        if k < 2:
            return group * rows + h * half, (2 * group + k) * width
        if k < 4:
            return 4 * rows, UP + (4 * h + 2 * group + k - 2) * width
        return 2 * rows + (2 * h + k - 4) * half, DN + group * width

    def spread(ref, group, h, k):
        row, place = places(group, h, k)
        row = row if isinstance(row, int) else pl.multiple_of(row, 16)
        at = pl.ds(pl.multiple_of(place, 16), width)
        return times(ref[pl.ds(row, half), :], top[at, :], low[at, :], ((1,), (1,)))

    vs, vr, vm = (vs_sq, vs_up, vs_dn), (vr_sq, vr_up, vr_dn), (vm_sq, vm_up, vm_dn)
    own, out = (o_sq, o_up, o_dn), (w_sq, w_up, w_dn)

    def update(group, h, k):
        outer = spread(mean, group, h, k)
        moment = piece(vm, 0, group, h, k)
        new_moment, weights = advance(piece(vs, 0, group, h, k)[...], moment[...], outer)
        moment[...] = new_moment
        piece(own, 0, group, h, k)[...] = weights

    def leave(group, h, k):
        delta = piece(vr, 0, group, h, k)
        delta[...] = delta[...] - spread(part, group, h, k)

    X, Y, Z = 0, 1, 2
    target = {X: (plane, side), Y: (plane, across), Z: (twin, me)}
    arrivals = {X: x_in, Y: y_in, Z: z_in}

    def send(way, kind, owner, group, h, k, mine=False):
        pltpu.make_async_remote_copy(
            piece(own, 0, group, h, k) if mine else piece(out, owner, group, h, k),
            piece(out, owner, group, h, k),
            link_out.at[way * 3 + k // 2],
            arrivals[way].at[kind * CHUNKS + k],
            device_id=target[way], device_id_type=MESH,
        ).start()

    def arrive(way, kind, owner, group, h, k):
        there = piece(out, owner, group, h, k)
        pltpu.make_async_copy(there, there, arrivals[way].at[kind * CHUNKS + k]).wait()
        pltpu.make_async_remote_copy(
            there, there, core_out.at[k // 2], core_in.at[k // 2],
            device_id=(plane, sibling), device_id_type=MESH,
        ).start()

    def first(k):
        update(b, 0, k)
        send(X, 0, me, b, 0, k, True)
        update(b, 1, k)
        send(Y, 0, me, b, 1, k, True)
        update(a, 1, k)
        send(X, 1, me, a, 1, k, True)
        update(a, 0, k)
        send(Y, 1, me, a, 0, k, True)

    def second(k):
        send(X, 3, me, a, 0, k, True)
        send(Y, 3, me, a, 1, k, True)

    for k in range(3):
        first(k)
    nm_value, ln_value = advance(s_ln[...], m_ln[...], mean[pl.ds(tail, 4), :][:, :rows])
    nm_ln[...] = nm_value
    o_ln[...] = jnp.zeros_like(o_ln)
    o_ln[:4, :rows] = ln_value
    norms = [
        pltpu.make_async_remote_copy(
            o_ln, w_ln.at[me], ln_out.at[i], ln_in.at[i],
            device_id=(plane, mate), device_id_type=MESH,
        )
        for i, mate in enumerate(mates)
    ]
    for copy in norms:
        copy.start()

    homes = (
        w_sq.at[:, pl.ds(pl.multiple_of(me * rows, 16), rows), :],
        w_up.at[pl.ds(pl.multiple_of(me * rows, 16), rows), :],
        w_dn.at[pl.ds(pl.multiple_of(me * deep, 16), deep), :],
    )
    kept = [pltpu.make_async_copy(own[i], homes[i], own_sem.at[i]) for i in range(3)]
    kept.append(pltpu.make_async_copy(o_ln, w_ln.at[me], own_sem.at[3]))
    stores = [
        pltpu.make_async_copy(src, dst, store_sem.at[i])
        for i, (src, dst) in enumerate([
            (vm_sq, nm_sq), (vm_up, nm_up), (vm_dn, nm_dn), (vr_sq, nr_sq), (vr_up, nr_up), (vr_dn, nr_dn),
        ])
    ]

    for k in range(CHUNKS + 2):
        if k < CHUNKS:
            arrive(X, 0, side, b, 0, k)
            send(Y, 2, side, b, 0, k)
            arrive(Y, 0, across, b, 1, k)
            send(X, 2, across, b, 1, k)
            arrive(X, 1, side, a, 1, k)
            send(Z, 2, side, a, 1, k)
            arrive(Y, 1, across, a, 0, k)
            send(Z, 3, across, a, 0, k)
        if 1 <= k <= CHUNKS:
            j = k - 1
            arrive(Y, 2, corner, b, 0, j)
            send(Z, 0, corner, b, 0, j)
            arrive(X, 2, corner, b, 1, j)
            send(Z, 1, corner, b, 1, j)
        if k + 3 < CHUNKS:
            first(k + 3)
        for j in {3: (0,), 4: (1, 2), 5: (3, 4, 5)}.get(k, ()):
            second(j)
        if k == 3:
            for i in range(3):
                kept[i].start()
                stores[i].start()
                pltpu.make_async_remote_copy(
                    own[i], homes[i], core_out.at[i], core_in.at[i],
                    device_id=(plane, sibling), device_id_type=MESH,
                ).start()
            kept[3].start()
        if k < CHUNKS:
            for group in range(2):
                for h in range(2):
                    leave(group, h, k)
            if k % 2:
                stores[3 + k // 2].start()

    for j in range(CHUNKS):
        arrive(Z, 2, side, b, 1, j)
        arrive(Z, 3, across, b, 0, j)
        arrive(Z, 0, corner, a, 0, j)
        arrive(Z, 1, corner, a, 1, j)
        arrive(X, 3, side, a, 0, j)
        arrive(Y, 3, across, a, 1, j)

    for i in range(3):
        for way in range(3):
            pltpu.make_async_copy(own[i], own[i], link_out.at[way * 3 + i]).wait()
        share_ = (w_sq.at[:, pl.ds(0, 4 * rows), :], w_up.at[pl.ds(0, 4 * rows), :], w_dn.at[pl.ds(0, 4 * deep), :])[i]
        pltpu.make_async_copy(share_, share_, core_out.at[i]).wait()
        pltpu.make_async_copy(share_, share_, core_in.at[i]).wait()
    for copy in kept + norms + stores:
        copy.wait()


def whole_step(trained, start, resid, moment, norms, bases, n):
    f32, bf16, dma = jnp.float32, jnp.bfloat16, pltpu.SemaphoreType.DMA
    shape = jax.ShapeDtypeStruct
    sq, up, dn = (x.shape for x in start)
    tall = 14 * sq[2]
    held = [pltpu.VMEM(x, f32) for x in (sq, up, dn)]
    results = pl.pallas_call(
        step_kernel,
        out_shape=[shape(x, f32) for x in (sq, up, dn, sq, up, dn, norms[0].shape)]
        + [
            shape((sq[0], n * sq[1], sq[2]), bf16),
            shape((n * up[0], up[1]), bf16),
            shape((n * dn[0], dn[1]), bf16),
            shape((n, 16, LANES), bf16),
        ],
        in_specs=[ANY] * 12 + [VMEM] * 6,
        out_specs=[ANY] * 6 + [VMEM] + [ANY] * 4,
        scratch_shapes=held * 4
        + [pltpu.VMEM(x, bf16) for x in (sq, up, dn, (16, LANES))]
        + [pltpu.VMEM((sq[2], LANES), f32), pltpu.VMEM((tall, LANES), bf16), pltpu.VMEM((tall, LANES), bf16)]
        + [pltpu.VMEM((448, LANES), f32), pltpu.VMEM((448, LANES), f32), pltpu.VMEM((3, 112, LANES), f32)]
        + [dma((12,)), dma((6,)), dma((3,)), dma((3,)), dma((3,)), dma((3,))]
        + [dma((4 * CHUNKS,))] * 3
        + [dma((9,)), dma((3,)), dma((3,)), dma((4,)), dma((7,)), dma((7,))],
        compiler_params=pltpu.CompilerParams(
            collective_id=1, has_side_effects=True, vmem_limit_bytes=56 * 2**20
        ),
        name="whole_step",
    )(*trained, *start, *resid, *moment, *norms, *bases)
    *rest, lns = results
    lns = lns[:, : norms[0].shape[0], : norms[0].shape[1]].transpose(1, 0, 2).reshape(norms[0].shape[0], -1)
    nr = [x[None] for x in rest[:3]]
    return (*nr, *rest[3:], lns)


def on_device(
    trained_sq,
    trained_up,
    trained_down,
    trained_ln,
    start_sq,
    start_up,
    start_down,
    start_ln,
    resid_sq,
    resid_up,
    resid_down,
    mom_sq,
    mom_up,
    mom_down,
    mom_ln,
    basis_sq,
    basis_up,
    basis_down,
):
    fine = lax.Precision.HIGH
    groups = lax.axis_size("rep")
    shards = lax.axis_size("shard")
    if shards == 8 and groups == 4 and basis_down.shape[1] * 2 == LANES:
        return whole_step(
            (trained_sq[0], trained_up[0], trained_down[0]),
            (start_sq, start_up, start_down),
            (resid_sq[0], resid_up[0], resid_down[0]),
            (mom_sq, mom_up, mom_down),
            (trained_ln[0], start_ln, mom_ln),
            tuple(jnp.swapaxes(x, -1, -2) for x in (basis_sq, basis_up, basis_down)),
            shards,
        )
    delta_sq = start_sq - trained_sq[0] + resid_sq[0]
    factor_sq = jnp.einsum("mrd,mdk->mrk", delta_sq, basis_sq, precision=fine)
    delta_up = start_up - trained_up[0] + resid_up[0]
    factor_up = jnp.dot(delta_up, basis_up, precision=fine, preferred_element_type=jnp.float32)
    delta_down = start_down - trained_down[0] + resid_down[0]
    factor_down = jnp.dot(delta_down, basis_down, precision=fine, preferred_element_type=jnp.float32)
    norm_delta = start_ln - trained_ln[0]

    parts = (factor_sq, factor_up, factor_down, norm_delta)
    flat = jnp.concatenate([part.reshape(-1) for part in parts])
    slot = -(-flat.size // (groups * 8 * LANES)) * 8
    flat = jnp.pad(flat, (0, groups * slot * LANES - flat.size))
    mean = mean_over_groups(flat.reshape(groups, slot, LANES), groups).reshape(-1)
    means, at = [], 0
    for part in parts:
        means.append(mean[at : at + part.size].reshape(part.shape))
        at += part.size
    mean_sq, mean_up, mean_down, mean_ln = means

    new_resid_sq = delta_sq - jnp.einsum("mrk,mdk->mrd", factor_sq, basis_sq, precision=fine)
    new_resid_up = delta_up - jnp.einsum("rk,fk->rf", factor_up, basis_up, precision=fine)
    new_resid_down = delta_down - jnp.einsum("rk,dk->rd", factor_down, basis_down, precision=fine)
    new_mom_ln, norm_weights = advance(start_ln, mom_ln, mean_ln)
    outer_sq = jnp.einsum("mrk,mdk->mrd", mean_sq, basis_sq, precision=fine)
    outer_up = jnp.einsum("rk,fk->rf", mean_up, basis_up, precision=fine)
    outer_down = jnp.einsum("rk,dk->rd", mean_down, basis_down, precision=fine)
    new_mom_sq, owned_sq = advance(start_sq, mom_sq, outer_sq)
    new_mom_up, owned_up = advance(start_up, mom_up, outer_up)
    new_mom_down, owned_down = advance(start_down, mom_down, outer_down)
    weights = (
        lax.all_gather(owned_sq, "shard", axis=1, tiled=True),
        lax.all_gather(owned_up, "shard", axis=0, tiled=True),
        lax.all_gather(owned_down, "shard", axis=0, tiled=True),
        lax.all_gather(norm_weights, "shard", axis=1, tiled=True),
    )
    return (
        new_resid_sq[None],
        new_resid_up[None],
        new_resid_down[None],
        new_mom_sq,
        new_mom_up,
        new_mom_down,
        new_mom_ln,
        *weights,
    )


def solution(mesh):
    placed = (
        P("rep", None, "shard", None),
        P("rep", "shard", None),
        P("rep", "shard", None),
        P("rep", None, "shard"),
        P(None, "shard", None),
        P("shard", None),
        P("shard", None),
        P(None, "shard"),
        P("rep", None, "shard", None),
        P("rep", "shard", None),
        P("rep", "shard", None),
        P(None, "shard", None),
        P("shard", None),
        P("shard", None),
        P(None, "shard"),
        P(),
        P(),
        P(),
    )
    return jax.shard_map(
        on_device,
        mesh=mesh,
        in_specs=placed,
        out_specs=(
            P("rep", None, "shard", None),
            P("rep", "shard", None),
            P("rep", "shard", None),
            P(None, "shard", None),
            P("shard", None),
            P("shard", None),
            P(None, "shard"),
            P(),
            P(),
            P(),
            P(),
        ),
        check_vma=False,
    )
```
